256 devices in a mesh: gx: 4 (over x), gy: 8 (over y, z_lo), gz: 8 (over z_hi, core).
Axes of the slice: x: 4, y: 4, z: 8 (z_hi: 4, z_lo: 2; z = z_hi * 2 + z_lo), core: 2. Of those that a mesh axis runs over, the one named last changes fastest.
Arguments:
- inputs: bfloat16 [1024, 6144], P(('gx', 'gy'), 'gz'), may hold values from -6 to 6
- weight_in: bfloat16 [6144, 24576], P('gz', ('gx', 'gy')), may hold values from -0.078125 to 0.078125
- weight_out: bfloat16 [24576, 6144], P(('gx', 'gy'), 'gz'), may hold values from -0.0390625 to 0.0390625
- output_grad: bfloat16 [1024, 6144], P(('gx', 'gy'), 'gz'), may hold values from -0.375 to 0.375
Outputs:
- output: bfloat16 [1024, 6144], P(('gx', 'gy'), 'gz')
- input_grad: bfloat16 [1024, 6144], P(('gx', 'gy'), 'gz')
- weight_in_grad: bfloat16 [6144, 24576], P('gz', ('gx', 'gy'))
- weight_out_grad: bfloat16 [24576, 6144], P(('gx', 'gy'), 'gz')
The draws below stay inside these ranges and needn't reach their ends.
All inputs are finite; a program needn't handle non-finite values.
Results may differ from the reference program's by a relative error of at most 0.0049.
Values may be sent and summed in bfloat16 or wider, within the bound.
No kernel may reach another device: no remote copies, remote signals or barrier semaphores. Data moves between devices by JAX's collectives and lax.ppermute only.
A program may use at most 128 MiB of HBM per device.

```python
import jax
import jax.numpy as jnp
from jax import lax

D = 6144
FF = 24576
TOKENS = 1024


def block_scale(own_key, extent, pieces, low, high):
    level = 1.0
    for dim, blocks in pieces:
        heights = jax.random.uniform(jax.random.fold_in(jax.random.fold_in(own_key, 6), dim), (blocks,), jnp.float32, low / len(pieces), high / len(pieces))
        level = level * jnp.repeat(jnp.exp(heights), extent[dim] // blocks).reshape((-1,) + (1,) * (len(extent) - 1 - dim))
    return level


def noise(own_key, extent, deviation, limit, cuts=(), held_as=jnp.bfloat16):
    result = deviation * jax.random.normal(own_key, extent, jnp.float32)
    if cuts:
        result = result * block_scale(own_key, extent, cuts, -0.22, 0.18)
    return jnp.clip(result, -limit, limit).astype(held_as)


def setup_inputs(seed: int = 0) -> dict:
    keys = jax.random.split(jax.random.key(seed), 5)
    inputs = noise(keys[0], (TOKENS, D), 1.0, 6.0, ((0, 32), (1, 8)))
    weight_in = noise(keys[1], (D, FF), D ** -0.5, 0.078125, ((0, 8), (1, 32)))
    weight_out = noise(keys[2], (FF, D), FF ** -0.5, 0.0390625, ((0, 32), (1, 8)))
    output_grad = noise(keys[3], (TOKENS, D), (TOKENS // 4) ** -0.5, 0.375, ((0, 32), (1, 8)))
    return {"inputs": inputs, "weight_in": weight_in, "weight_out": weight_out, "output_grad": output_grad}


def gelu_value(value):
    inner = 0.7978845608 * (value + 0.044715 * value * value * value)
    return 0.5 * value * (1.0 + jnp.tanh(inner))


def gelu_slope(value):
    inner = 0.7978845608 * (value + 0.044715 * value * value * value)
    tangent = jnp.tanh(inner)
    return 0.5 * (1.0 + tangent) + 0.5 * value * (1.0 - tangent * tangent) * 0.7978845608 * (1.0 + 0.134145 * value * value)


def against(left, right):
    return lax.dot_general(left, right, (((1,), (1,)), ((), ())), preferred_element_type=jnp.float32)


def across(left, right):
    return lax.dot_general(left, right, (((0,), (0,)), ((), ())), preferred_element_type=jnp.float32)


def reference(inputs, weight_in, weight_out, output_grad):
    preact = jnp.dot(inputs, weight_in, preferred_element_type=jnp.float32)
    hidden = gelu_value(preact).astype(jnp.bfloat16)
    output = jnp.dot(hidden, weight_out, preferred_element_type=jnp.float32).astype(jnp.bfloat16)
    grad_hidden = against(output_grad, weight_out)
    grad_pre = (grad_hidden * gelu_slope(preact)).astype(jnp.bfloat16)
    input_grad = against(grad_pre, weight_in).astype(jnp.bfloat16)
    weight_in_grad = across(inputs, grad_pre).astype(jnp.bfloat16)
    weight_out_grad = across(hidden, output_grad).astype(jnp.bfloat16)
    return output, input_grad, weight_in_grad, weight_out_grad
```

```python
import jax
import jax.numpy as jnp
from jax import lax
from jax.sharding import PartitionSpec as P

F32 = jnp.float32
BF16 = jnp.bfloat16
ROWS = ("gx", "gy")


def gelu_both(value):
    inner = 0.7978845608 * (value + 0.044715 * value * value * value)
    tangent = jnp.tanh(inner)
    slope = 0.5 * (1.0 + tangent) + 0.5 * value * (1.0 - tangent * tangent) * 0.7978845608 * (
        1.0 + 0.134145 * value * value
    )
    return 0.5 * value * (1.0 + tangent), slope


def product(left, right):
    return jnp.dot(left, right, preferred_element_type=F32)


def against(left, right):
    return lax.dot_general(left, right, (((1,), (1,)), ((), ())), preferred_element_type=F32)


def across(left, right):
    return lax.dot_general(left, right, (((0,), (0,)), ((), ())), preferred_element_type=F32)


def gather_rows(block, peers):
    copies = jnp.broadcast_to(block[None], (peers,) + block.shape)
    return lax.all_to_all(copies, ROWS, 0, 0).reshape(-1, block.shape[1])


def scatter_rows(partial, peers):
    pieces = partial.astype(BF16).reshape(peers, -1, partial.shape[1])
    return lax.all_to_all(pieces, ROWS, 0, 0).astype(F32).sum(0).astype(BF16)


def on_device(inputs, weight_in, weight_out, output_grad):
    peers = lax.axis_size("gx") * lax.axis_size("gy")
    depth = lax.axis_size("gz")
    ring = depth // 2
    place = lax.axis_index("gz")
    core = place % 2
    spot = place // 2
    tokens = peers * inputs.shape[0]
    half = tokens // 2
    quarter = half // ring
    split = quarter // 2

    def step(block, hops):
        pairs = [(i, ((i // 2 + hops) % ring) * 2 + i % 2) for i in range(depth)]
        return lax.ppermute(block, "gz", pairs)

    def swap(block):
        return lax.ppermute(block, "gz", [(i, i ^ 1) for i in range(depth)])

    def pick(array, index):
        return lax.dynamic_index_in_dim(array, index, 0, keepdims=False)

    def reduce_features(left, multiply):
        halves = left.reshape(2, half, -1)
        away = swap(multiply(pick(halves, 1 - core)).astype(BF16))
        total = multiply(pick(halves, core)) + away.astype(F32)
        blocks = total.reshape(ring, quarter, -1)
        own, ahead, far, behind = (pick(blocks, (spot + d) % ring) for d in range(4))
        far = far.astype(BF16)
        up = step(far[:split], 1)
        down = step(far[split:], -1)
        ahead = jnp.concatenate([ahead[:split] + up.astype(F32), ahead[split:]], 0).astype(BF16)
        behind = jnp.concatenate([behind[:split], behind[split:] + down.astype(F32)], 0).astype(BF16)
        return own + step(ahead, 1).astype(F32) + step(behind, -1).astype(F32)

    def gather_tokens(block):
        up = step(block, 1)
        down = step(block, -1)
        far = jnp.concatenate([step(up[:split], 1), step(down[split:], -1)], 0)
        mine = jnp.zeros((ring, quarter, block.shape[1]), block.dtype)
        for offset, piece in ((0, block), (-1, up), (1, down), (2, far)):
            mine = lax.dynamic_update_index_in_dim(mine, piece, (spot + offset) % ring, 0)
        mine = mine.reshape(half, -1)
        other = swap(mine)
        first = jnp.where(core == 0, mine, other)
        second = jnp.where(core == 0, other, mine)
        return jnp.concatenate([first, second], 0)

    input_all = gather_rows(inputs, peers)
    preact = reduce_features(input_all, lambda rows: product(rows, weight_in))
    grad_all = gather_rows(output_grad, peers)
    hidden, slope = gelu_both(preact)
    hidden_all = gather_tokens(hidden.astype(BF16))
    grad_hidden = reduce_features(grad_all, lambda rows: against(rows, weight_out))
    grad_pre_all = gather_tokens((grad_hidden * slope).astype(BF16))
    output = scatter_rows(product(hidden_all, weight_out), peers)
    input_grad = scatter_rows(against(grad_pre_all, weight_in), peers)
    weight_out_grad = across(hidden_all, grad_all).astype(BF16)
    weight_in_grad = across(input_all, grad_pre_all).astype(BF16)
    return (output, input_grad, weight_in_grad, weight_out_grad)


def solution(mesh):
    rows = P(("gx", "gy"), "gz")
    columns = P("gz", ("gx", "gy"))
    return jax.shard_map(
        on_device,
        mesh=mesh,
        in_specs=(rows, columns, rows, rows),
        out_specs=(rows, rows, columns, rows),
        check_vma=False,
    )
```

```python
import functools

import jax
import jax.numpy as jnp
from jax import lax
from jax.experimental import pallas as pl
from jax.experimental.pallas import tpu as pltpu
from jax.sharding import Mesh, PartitionSpec as P

F32 = jnp.float32
BF16 = jnp.bfloat16
NEAR = ("x", "l")
FAR = ("y", "x", "l")
VMEM = 32 * 2**20


def gelu_both(value):
    inner = 0.7978845608 * (value + 0.044715 * value * value * value)
    tangent = jnp.tanh(inner)
    slope = 0.5 * (1.0 + tangent) + 0.5 * value * (1.0 - tangent * tangent) * 0.7978845608 * (
        1.0 + 0.134145 * value * value
    )
    return 0.5 * value * (1.0 + tangent), slope


def across(left, right):
    return lax.dot_general(left, right, (((0,), (0,)), ((), ())), preferred_element_type=F32)


def move(block, axis, hops):
    size = lax.axis_size(axis)
    return lax.ppermute(block, axis, [(i, (i + hops) % size) for i in range(size)])


def pick(array, index):
    return lax.dynamic_index_in_dim(array, index, 0, keepdims=False)


def ring_gather(block, axis):
    spot = lax.axis_index(axis)
    cut = block.shape[0] // 2
    up = move(block, axis, 1)
    down = move(block, axis, -1)
    far_up = move(up[:cut], axis, 1)
    far_down = move(down[cut:], axis, -1)
    whole = jnp.zeros((4,) + block.shape, block.dtype)
    for hops, piece in ((0, block), (3, up), (1, down)):
        whole = lax.dynamic_update_index_in_dim(whole, piece, (spot + hops) % 4, 0)
    far = (spot + 2) % 4
    whole = lax.dynamic_update_slice(whole, far_up[None], (far, 0, 0))
    whole = lax.dynamic_update_slice(whole, far_down[None], (far, cut, 0))
    return whole.reshape(-1, block.shape[1])


def ring_sum(blocks, axis):
    spot = lax.axis_index(axis)
    cut = blocks.shape[1] // 2
    own, ahead, far, behind = (pick(blocks, (spot + d) % 4) for d in range(4))
    far = far.astype(BF16)
    up = move(far[:cut], axis, 1).astype(F32)
    down = move(far[cut:], axis, -1).astype(F32)
    ahead = jnp.concatenate([ahead[:cut] + up, ahead[cut:]], 0).astype(BF16)
    behind = jnp.concatenate([behind[:cut], behind[cut:] + down], 0).astype(BF16)
    return own + move(ahead, axis, 1).astype(F32) + move(behind, axis, -1).astype(F32)


def product_kernel(turned, which_ref, rows_ref, weight_ref, out_ref):
    sides = ((1,), (1,)) if turned else ((1,), (0,))
    out_ref[...] = lax.dot_general(
        rows_ref[...], weight_ref[...], (sides, ((), ())), preferred_element_type=F32
    ).astype(out_ref.dtype)


def product(rows, weight, turned, dtype, tile, which=None, weigh=1):
    if which is None:
        stride, which = 1, jnp.zeros((1,), jnp.int32)
    else:
        stride, which = 2, which.astype(jnp.int32).reshape(1)
    steps = rows.shape[0] // tile // stride
    width = weight.shape[0] if turned else weight.shape[1]
    return pl.pallas_call(
        functools.partial(product_kernel, turned),
        grid_spec=pltpu.PrefetchScalarGridSpec(
            num_scalar_prefetch=1,
            grid=(steps,),
            in_specs=[
                pl.BlockSpec((tile, rows.shape[1]), lambda i, which: (stride * i + which[0], 0)),
                pl.BlockSpec(weight.shape, lambda i, which: (0, 0)),
            ],
            out_specs=pl.BlockSpec((tile, width), lambda i, which: (i, 0)),
        ),
        out_shape=jax.ShapeDtypeStruct((steps * tile, width), dtype),
        compiler_params=pltpu.CompilerParams(vmem_limit_bytes=VMEM),
        cost_estimate=pl.CostEstimate(
            flops=2 * weigh * steps * tile * weight.size,
            bytes_accessed=2 * (steps * tile * rows.shape[1] + weight.size) + 4 * steps * tile * width,
            transcendentals=0,
        ),
    )(which, rows, weight)


def on_device(inputs, weight_in, weight_out, output_grad):
    core = lax.axis_index("c")
    rows, features = inputs.shape
    near = lax.axis_size(NEAR)
    peers = lax.axis_size(FAR)
    tokens = peers * rows
    ring = lax.axis_size("h")
    tile = tokens // (2 * ring)

    def pair_sum(left, weight, turned):
        away = move(product(left, weight, turned, BF16, tile, 1 - core), "c", 1)
        total = product(left, weight, turned, F32, tile, core) + away.astype(F32)
        return total.reshape(ring, tile, -1)

    def rows_sum(partial):
        pieces = lax.all_to_all(partial.reshape(peers, rows, -1), FAR, 0, 0)
        return pieces.astype(F32).sum(0).astype(BF16)

    both = jnp.concatenate([inputs, output_grad], 1)
    both = lax.all_to_all(jnp.broadcast_to(both[None], (near,) + both.shape), NEAR, 0, 0)
    both = both.reshape(near * rows, -1)
    grad_all = lax.all_gather(both[:, features:], "y", axis=0, tiled=True)
    input_all = ring_gather(both[:, :features], "y")

    preact = ring_sum(pair_sum(input_all, weight_in, False), "h")
    pairs = pair_sum(grad_all, weight_out, True)
    hidden = gelu_both(preact)[0].astype(BF16)
    mine = ring_gather(hidden, "h").reshape(ring, 1, tile, -1)
    other = move(mine, "c", 1)
    hidden_all = jnp.concatenate(
        [jnp.where(core == 0, mine, other), jnp.where(core == 0, other, mine)], 1
    ).reshape(tokens, -1)
    grad_hidden = ring_sum(pairs, "h")
    grad_hidden, preact = lax.optimization_barrier((grad_hidden, preact))
    grad_pre = (grad_hidden * gelu_both(preact)[1]).astype(BF16)
    grad_pre_all = lax.all_gather(grad_pre, ("h", "c"), axis=0, tiled=True)

    ready = lax.optimization_barrier((hidden_all, grad_pre))[0]
    output = rows_sum(jnp.dot(ready, weight_out, preferred_element_type=F32).astype(BF16))
    input_grad = rows_sum(product(grad_pre_all, weight_in, True, BF16, 2 * tile, weigh=40))
    weight_out_grad = across(hidden_all, grad_all).astype(BF16)
    weight_in_grad = across(input_all, grad_pre_all).astype(BF16)
    return (output, input_grad, weight_in_grad, weight_out_grad)


def solution(mesh):
    fine = Mesh(mesh.devices.reshape(4, 4, 2, 4, 2), ("x", "y", "l", "h", "c"))
    rows = P(("x", "y", "l"), ("h", "c"))
    columns = P(("h", "c"), ("x", "y", "l"))
    return jax.shard_map(
        on_device,
        mesh=fine,
        in_specs=(rows, columns, rows, rows),
        out_specs=(rows, rows, columns, rows),
        check_vma=False,
    )
```

```python
import functools

import jax
import jax.numpy as jnp
from jax import lax
from jax.experimental import pallas as pl
from jax.experimental.pallas import tpu as pltpu
from jax.sharding import Mesh, PartitionSpec as P

F32 = jnp.float32
BF16 = jnp.bfloat16
NEAR = ("x", "l")
FAR = ("y", "x", "l")
VMEM = 32 * 2**20


def gelu_both(value):
    inner = 0.7978845608 * (value + 0.044715 * value * value * value)
    tangent = jnp.tanh(inner)
    slope = 0.5 * (1.0 + tangent) + 0.5 * value * (1.0 - tangent * tangent) * 0.7978845608 * (
        1.0 + 0.134145 * value * value
    )
    return 0.5 * value * (1.0 + tangent), slope


def across(left, right):
    return lax.dot_general(left, right, (((0,), (0,)), ((), ())), preferred_element_type=F32)


def move(block, axis, hops):
    size = lax.axis_size(axis)
    return lax.ppermute(block, axis, [(i, (i + hops) % size) for i in range(size)])


def pick(array, index):
    return lax.dynamic_index_in_dim(array, index, 0, keepdims=False)


def ring_split(blocks, axis):
    spot = lax.axis_index(axis)
    own, ahead, far, behind = (pick(blocks, (spot + d) % 4) for d in range(4))
    return own, ahead, far.astype(BF16), behind


def both_ways(up, down, axis):
    return move(up, axis, 1), move(down, axis, -1)


def add_first(block, part):
    cut = part.shape[0]
    return jnp.concatenate([block[:cut] + part.astype(F32), block[cut:]], 0).astype(BF16)


def add_last(block, part):
    cut = block.shape[0] - part.shape[0]
    return jnp.concatenate([block[:cut], block[cut:] + part.astype(F32)], 0).astype(BF16)


def stack(*parts):
    return jnp.concatenate(parts, 0)


def ring_place(block, up, down, far_up, far_down, axis):
    spot = lax.axis_index(axis)
    cut = far_up.shape[0]
    whole = jnp.zeros((4,) + block.shape, block.dtype)
    for hops, piece in ((0, block), (3, up), (1, down)):
        whole = lax.dynamic_update_index_in_dim(whole, piece, (spot + hops) % 4, 0)
    far = (spot + 2) % 4
    whole = lax.dynamic_update_slice(whole, far_up[None], (far, 0, 0))
    return lax.dynamic_update_slice(whole, far_down[None], (far, cut, 0))


def product_kernel(turned, which_ref, rows_ref, weight_ref, *refs):
    out_ref = refs[-1]
    sides = ((1,), (1,)) if turned else ((1,), (0,))
    out_ref[...] = lax.dot_general(
        rows_ref[...], weight_ref[...], (sides, ((), ())), preferred_element_type=F32
    ).astype(out_ref.dtype)


def product(rows, weight, turned, dtype, tile, which=None, weigh=1, later=()):
    if which is None:
        stride, which = 1, jnp.zeros((1,), jnp.int32)
    else:
        stride, which = 2, which.astype(jnp.int32).reshape(1)
    steps = rows.shape[0] // tile // stride
    width = weight.shape[0] if turned else weight.shape[1]
    return pl.pallas_call(
        functools.partial(product_kernel, turned),
        grid_spec=pltpu.PrefetchScalarGridSpec(
            num_scalar_prefetch=1,
            grid=(steps,),
            in_specs=[
                pl.BlockSpec((tile, rows.shape[1]), lambda i, which: (stride * i + which[0], 0)),
                pl.BlockSpec(weight.shape, lambda i, which: (0, 0)),
            ]
            + [pl.BlockSpec(memory_space=pl.ANY)] * len(later),
            out_specs=pl.BlockSpec((tile, width), lambda i, which: (i, 0)),
        ),
        out_shape=jax.ShapeDtypeStruct((steps * tile, width), dtype),
        compiler_params=pltpu.CompilerParams(vmem_limit_bytes=VMEM),
        cost_estimate=pl.CostEstimate(
            flops=2 * weigh * steps * tile * weight.size,
            bytes_accessed=2 * (steps * tile * rows.shape[1] + weight.size) + 4 * steps * tile * width,
            transcendentals=0,
        ),
    )(which, rows, weight, *later)


def joined_kernel(turned, place_ref, mine_ref, other_ref, weight_ref, *refs):
    out_ref, rows_ref = refs[-2:]
    sides = ((1,), (1,)) if turned else ((1,), (0,))
    rows_ref[...] = jnp.where(pl.program_id(0) % 2 == 0, mine_ref[...], other_ref[...])
    out_ref[...] = lax.dot_general(
        rows_ref[...], weight_ref[...], (sides, ((), ())), preferred_element_type=F32
    ).astype(out_ref.dtype)


def joined_product(mine, other, weight, turned, place, later=()):
    tile = mine.shape[0] // 4
    width = weight.shape[0] if turned else weight.shape[1]

    def spread(i, place):
        return (place[0] + i // 2) % 4 * 2 + (place[1] + i) % 2, 0

    return pl.pallas_call(
        functools.partial(joined_kernel, turned),
        grid_spec=pltpu.PrefetchScalarGridSpec(
            num_scalar_prefetch=1,
            grid=(8,),
            in_specs=[pl.BlockSpec((tile, mine.shape[1]), lambda i, place: (i // 2, 0))] * 2
            + [pl.BlockSpec(weight.shape, lambda i, place: (0, 0))]
            + [pl.BlockSpec(memory_space=pl.ANY)] * len(later),
            out_specs=[pl.BlockSpec((tile, width), spread), pl.BlockSpec((tile, mine.shape[1]), spread)],
        ),
        out_shape=[
            jax.ShapeDtypeStruct((8 * tile, width), BF16),
            jax.ShapeDtypeStruct((8 * tile, mine.shape[1]), BF16),
        ],
        compiler_params=pltpu.CompilerParams(vmem_limit_bytes=VMEM),
        cost_estimate=pl.CostEstimate(
            flops=16 * tile * weight.size,
            bytes_accessed=2 * (2 * mine.size + weight.size) + 16 * tile * (width + mine.shape[1]),
            transcendentals=0,
        ),
    )(place, mine, other, weight, *later)


def local(kernel, outs, args, later=()):
    def body(*refs):
        kernel(*refs[: len(args)], *refs[len(args) + len(later) :])

    return pl.pallas_call(
        body,
        in_specs=[pl.BlockSpec(memory_space=pltpu.VMEM)] * len(args) + [pl.BlockSpec(memory_space=pl.ANY)] * len(later),
        out_specs=[pl.BlockSpec(memory_space=pltpu.VMEM)] * len(outs),
        out_shape=outs,
        compiler_params=pltpu.CompilerParams(vmem_limit_bytes=VMEM),
    )(*args, *later)


def pass_on(ahead_ref, up_ref, behind_ref, down_ref, up_out, down_out):
    cut = up_ref.shape[0]
    up_out[:cut] = (ahead_ref[:cut] + up_ref[...].astype(F32)).astype(BF16)
    up_out[cut:] = ahead_ref[cut:].astype(BF16)
    down_out[:cut] = behind_ref[:cut].astype(BF16)
    down_out[cut:] = (behind_ref[cut:] + down_ref[...].astype(F32)).astype(BF16)


def activate(own_ref, up_ref, down_ref, hidden_ref, slope_ref):
    hidden, slope = gelu_both(own_ref[...] + up_ref[...].astype(F32) + down_ref[...].astype(F32))
    hidden_ref[...] = hidden.astype(BF16)
    slope_ref[...] = slope


def weigh_slope(own_ref, up_ref, down_ref, slope_ref, out_ref):
    total = own_ref[...] + up_ref[...].astype(F32) + down_ref[...].astype(F32)
    out_ref[...] = (total * slope_ref[...]).astype(BF16)


def on_device(inputs, weight_in, weight_out, output_grad):
    core = lax.axis_index("c")
    rows, features = inputs.shape
    near = lax.axis_size(NEAR)
    peers = lax.axis_size(FAR)
    tokens = peers * rows
    ring = lax.axis_size("h")
    tile = tokens // (2 * ring)

    def pair_sum(left, weight, turned, later=(), last=()):
        away = move(product(left, weight, turned, BF16, tile, 1 - core, later=later), "c", 1)
        total = product(left, weight, turned, F32, tile, core, later=last) + away.astype(F32)
        return total.reshape(ring, tile, -1)

    def rows_sum(partial):
        pieces = lax.all_to_all(partial.reshape(peers, rows, -1), FAR, 0, 0)
        return pieces.astype(F32).sum(0).astype(BF16)

    def copies(block, axes):
        size = lax.axis_size(axes)
        sent = jnp.broadcast_to(block[None], (size,) + block.shape)
        return lax.all_to_all(sent, axes, 0, 0).reshape(size * rows, -1)

    def wire(count):
        return jax.ShapeDtypeStruct((count, units), BF16)

    units = weight_in.shape[1]
    cut = tile // 2
    input_all = copies(inputs, FAR)
    output_grad, input_all = lax.optimization_barrier((output_grad, input_all))
    grad = copies(output_grad, NEAR)

    own, ahead, far, behind = ring_split(pair_sum(input_all, weight_in, False), "h")
    up, down = both_ways(far[:cut], far[cut:], "h")
    grad_up, grad_down = both_ways(grad, grad, "y")
    ahead, behind = local(pass_on, [wire(tile)] * 2, (ahead, up, behind, down), (grad_up, grad_down))
    up, down = both_ways(ahead, behind, "h")
    part = grad.shape[0] // 2
    grad_far = both_ways(grad_up[:part], grad_down[part:], "y")
    hidden, slope = local(
        activate, [wire(tile), jax.ShapeDtypeStruct((tile, units), F32)], (own, up, down), grad_far
    )
    grad_all = ring_place(grad, grad_up, grad_down, *grad_far, "y").reshape(tokens, -1)

    up, down = both_ways(hidden, hidden, "h")
    own, ahead, far, behind = ring_split(pair_sum(grad_all, weight_out, True, (hidden,)), "h")
    far_up, far_down = both_ways(stack(far[:cut], up[:cut]), stack(far[cut:], down[cut:]), "h")
    mine = stack(hidden, down, far_up[cut:], far_down[cut:], up)
    other = move(mine, "c", 1)
    ahead, behind = local(pass_on, [wire(tile)] * 2, (ahead, far_up[:cut], behind, far_down[:cut]))
    up, down = both_ways(ahead, behind, "h")
    (grad_pre,) = local(weigh_slope, [wire(tile)], (own, up, down, slope), (other,))
    up, down = both_ways(grad_pre, grad_pre, "h")
    place = jnp.stack([lax.axis_index("h"), core]).astype(jnp.int32)
    partial, hidden_all = joined_product(mine, other, weight_out, False, place)
    far_up, far_down = both_ways(up[:cut], down[cut:], "h")
    partial, far_up, far_down = lax.optimization_barrier((partial, far_up, far_down))
    output = rows_sum(partial)
    mine_late = stack(grad_pre, down, far_up, far_down, up)
    other_late = move(mine_late, "c", 1)
    partial, grad_pre_all = joined_product(mine_late, other_late, weight_in, True, place)
    input_grad = rows_sum(partial)
    weight_out_grad = across(hidden_all, grad_all).astype(BF16)
    weight_in_grad = across(input_all, grad_pre_all).astype(BF16)
    return (output, input_grad, weight_in_grad, weight_out_grad)


def solution(mesh):
    fine = Mesh(mesh.devices.reshape(4, 4, 2, 4, 2), ("x", "y", "l", "h", "c"))
    rows = P(("x", "y", "l"), ("h", "c"))
    columns = P(("h", "c"), ("x", "y", "l"))
    return jax.shard_map(
        on_device,
        mesh=fine,
        in_specs=(rows, columns, rows, rows),
        out_specs=(rows, rows, columns, rows),
        check_vma=False,
    )
```

```python
import functools

import jax
import jax.numpy as jnp
from jax import lax
from jax.experimental import pallas as pl
from jax.experimental.pallas import tpu as pltpu
from jax.sharding import Mesh, PartitionSpec as P

F32 = jnp.float32
BF16 = jnp.bfloat16
NEAR = ("x", "l")
FAR = ("y", "x", "l")
VMEM = 32 * 2**20


def gelu_both(value):
    inner = 0.7978845608 * (value + 0.044715 * value * value * value)
    tangent = jnp.tanh(inner)
    slope = 0.5 * (1.0 + tangent) + 0.5 * value * (1.0 - tangent * tangent) * 0.7978845608 * (
        1.0 + 0.134145 * value * value
    )
    return 0.5 * value * (1.0 + tangent), slope


def across(left, right):
    return lax.dot_general(left, right, (((0,), (0,)), ((), ())), preferred_element_type=F32)


def move(block, axis, hops):
    size = lax.axis_size(axis)
    return lax.ppermute(block, axis, [(i, (i + hops) % size) for i in range(size)])


def pick(array, index):
    return lax.dynamic_index_in_dim(array, index, 0, keepdims=False)


def ring_split(blocks, axis):
    spot = lax.axis_index(axis)
    own, ahead, far, behind = (pick(blocks, (spot + d) % 4) for d in range(4))
    return own, ahead, far.astype(BF16), behind


def both_ways(up, down, axis):
    return move(up, axis, 1), move(down, axis, -1)


def add_first(block, part):
    cut = part.shape[0]
    return jnp.concatenate([block[:cut] + part.astype(F32), block[cut:]], 0).astype(BF16)


def add_last(block, part):
    cut = block.shape[0] - part.shape[0]
    return jnp.concatenate([block[:cut], block[cut:] + part.astype(F32)], 0).astype(BF16)


def stack(*parts):
    return jnp.concatenate(parts, 0)


def ring_place(block, up, down, far_up, far_down, axis):
    spot = lax.axis_index(axis)
    cut = far_up.shape[0]
    whole = jnp.zeros((4,) + block.shape, block.dtype)
    for hops, piece in ((0, block), (3, up), (1, down)):
        whole = lax.dynamic_update_index_in_dim(whole, piece, (spot + hops) % 4, 0)
    far = (spot + 2) % 4
    whole = lax.dynamic_update_slice(whole, far_up[None], (far, 0, 0))
    return lax.dynamic_update_slice(whole, far_down[None], (far, cut, 0))


def product_kernel(turned, which_ref, rows_ref, weight_ref, *refs):
    out_ref = refs[-1]
    sides = ((1,), (1,)) if turned else ((1,), (0,))
    out_ref[...] = lax.dot_general(
        rows_ref[...], weight_ref[...], (sides, ((), ())), preferred_element_type=F32
    ).astype(out_ref.dtype)


def product(rows, weight, turned, dtype, tile, which=None, weigh=1, later=()):
    if which is None:
        stride, which = 1, jnp.zeros((1,), jnp.int32)
    else:
        stride, which = 2, which.astype(jnp.int32).reshape(1)
    steps = rows.shape[0] // tile // stride
    width = weight.shape[0] if turned else weight.shape[1]
    return pl.pallas_call(
        functools.partial(product_kernel, turned),
        grid_spec=pltpu.PrefetchScalarGridSpec(
            num_scalar_prefetch=1,
            grid=(steps,),
            in_specs=[
                pl.BlockSpec((tile, rows.shape[1]), lambda i, which: (stride * i + which[0], 0)),
                pl.BlockSpec(weight.shape, lambda i, which: (0, 0)),
            ]
            + [pl.BlockSpec(memory_space=pl.ANY)] * len(later),
            out_specs=pl.BlockSpec((tile, width), lambda i, which: (i, 0)),
        ),
        out_shape=jax.ShapeDtypeStruct((steps * tile, width), dtype),
        compiler_params=pltpu.CompilerParams(vmem_limit_bytes=VMEM),
        cost_estimate=pl.CostEstimate(
            flops=2 * weigh * steps * tile * weight.size,
            bytes_accessed=weigh * (2 * (steps * tile * rows.shape[1] + weight.size) + 4 * steps * tile * width),
            transcendentals=0,
        ),
    )(which, rows, weight, *later)


def joined_kernel(turned, place_ref, mine_ref, other_ref, weight_ref, *refs):
    out_ref, rows_ref = refs[-2:]
    sides = ((1,), (1,)) if turned else ((1,), (0,))
    rows_ref[...] = jnp.where(pl.program_id(0) % 2 == 0, mine_ref[...], other_ref[...])
    out_ref[...] = lax.dot_general(
        rows_ref[...], weight_ref[...], (sides, ((), ())), preferred_element_type=F32
    ).astype(out_ref.dtype)


def joined_product(mine, other, weight, turned, place, later=()):
    tile = mine.shape[0] // 4
    width = weight.shape[0] if turned else weight.shape[1]

    def spread(i, place):
        return (place[0] + i // 2) % 4 * 2 + (place[1] + i) % 2, 0

    return pl.pallas_call(
        functools.partial(joined_kernel, turned),
        grid_spec=pltpu.PrefetchScalarGridSpec(
            num_scalar_prefetch=1,
            grid=(8,),
            in_specs=[pl.BlockSpec((tile, mine.shape[1]), lambda i, place: (i // 2, 0))] * 2
            + [pl.BlockSpec(weight.shape, lambda i, place: (0, 0))]
            + [pl.BlockSpec(memory_space=pl.ANY)] * len(later),
            out_specs=[pl.BlockSpec((tile, width), spread), pl.BlockSpec((tile, mine.shape[1]), spread)],
        ),
        out_shape=[
            jax.ShapeDtypeStruct((8 * tile, width), BF16),
            jax.ShapeDtypeStruct((8 * tile, mine.shape[1]), BF16),
        ],
        compiler_params=pltpu.CompilerParams(vmem_limit_bytes=VMEM),
        cost_estimate=pl.CostEstimate(
            flops=16 * tile * weight.size,
            bytes_accessed=2 * (2 * mine.size + weight.size) + 16 * tile * (width + mine.shape[1]),
            transcendentals=0,
        ),
    )(place, mine, other, weight, *later)


def local(kernel, outs, args, later=(), flops=0):
    def body(*refs):
        kernel(*refs[: len(args)], *refs[len(args) + len(later) :])

    return pl.pallas_call(
        body,
        in_specs=[pl.BlockSpec(memory_space=pltpu.VMEM)] * len(args) + [pl.BlockSpec(memory_space=pl.ANY)] * len(later),
        out_specs=[pl.BlockSpec(memory_space=pltpu.VMEM)] * len(outs),
        out_shape=outs,
        compiler_params=pltpu.CompilerParams(vmem_limit_bytes=VMEM),
        cost_estimate=pl.CostEstimate(flops=flops, bytes_accessed=0, transcendentals=0) if flops else None,
    )(*args, *later)


def pass_on(ahead_ref, up_ref, behind_ref, down_ref, up_out, down_out):
    cut = up_ref.shape[0]
    up_out[:cut] = (ahead_ref[:cut] + up_ref[...].astype(F32)).astype(BF16)
    up_out[cut:] = ahead_ref[cut:].astype(BF16)
    down_out[:cut] = behind_ref[:cut].astype(BF16)
    down_out[cut:] = (behind_ref[cut:] + down_ref[...].astype(F32)).astype(BF16)


def activate(own_ref, up_ref, down_ref, hidden_ref, slope_ref):
    hidden, slope = gelu_both(own_ref[...] + up_ref[...].astype(F32) + down_ref[...].astype(F32))
    hidden_ref[...] = hidden.astype(BF16)
    slope_ref[...] = slope


def weigh_slope(own_ref, up_ref, down_ref, slope_ref, out_ref):
    total = own_ref[...] + up_ref[...].astype(F32) + down_ref[...].astype(F32)
    out_ref[...] = (total * slope_ref[...]).astype(BF16)


def on_device(inputs, weight_in, weight_out, output_grad):
    core = lax.axis_index("c")
    rows, features = inputs.shape
    near = lax.axis_size(NEAR)
    peers = lax.axis_size(FAR)
    tokens = peers * rows
    ring = lax.axis_size("h")
    tile = tokens // (2 * ring)

    def pair_sum(left, weight, turned, later=(), last=(), weigh=1):
        away = move(product(left, weight, turned, BF16, tile, 1 - core, weigh, later), "c", 1)
        total = product(left, weight, turned, F32, tile, core, weigh, last) + away.astype(F32)
        return total.reshape(ring, tile, -1)

    def rows_sum(partial):
        pieces = lax.all_to_all(partial.reshape(peers, rows, -1), FAR, 0, 0)
        return pieces.astype(F32).sum(0).astype(BF16)

    def copies(block, axes):
        size = lax.axis_size(axes)
        sent = jnp.broadcast_to(block[None], (size,) + block.shape)
        return lax.all_to_all(sent, axes, 0, 0).reshape(size * rows, -1)

    def wire(count):
        return jax.ShapeDtypeStruct((count, units), BF16)

    units = weight_in.shape[1]
    cut = tile // 2
    input_all = copies(inputs, FAR)
    output_grad, input_all = lax.optimization_barrier((output_grad, input_all))
    grad = copies(output_grad, NEAR)

    own, ahead, far, behind = ring_split(pair_sum(input_all, weight_in, False), "h")
    up, down = both_ways(far[:cut], far[cut:], "h")
    grad_up, grad_down = both_ways(grad, grad, "y")
    ahead, behind = local(pass_on, [wire(tile)] * 2, (ahead, up, behind, down), (grad_up, grad_down))
    up, down = both_ways(ahead, behind, "h")
    part = grad.shape[0] // 2
    grad_far = both_ways(grad_up[:part], grad_down[part:], "y")
    hidden, slope = local(
        activate, [wire(tile), jax.ShapeDtypeStruct((tile, units), F32)], (own, up, down), (), 2 * 10**10
    )
    grad_all = ring_place(grad, grad_up, grad_down, *grad_far, "y").reshape(tokens, -1)

    own, ahead, far, behind = ring_split(pair_sum(grad_all, weight_out, True, (ahead, behind), (), 0), "h")
    up, down = both_ways(stack(hidden, far[:cut]), stack(hidden, far[cut:]), "h")
    ahead, behind = local(pass_on, [wire(tile)] * 2, (ahead, up[tile:], behind, down[tile:]))
    far_up, far_down = both_ways(stack(ahead, up[:cut]), stack(behind, down[cut:tile]), "h")
    mine = stack(hidden, down[:tile], far_up[tile:], far_down[tile:], up[:tile])
    other = move(mine, "c", 1)
    (grad_pre,) = local(weigh_slope, [wire(tile)], (own, far_up[:tile], far_down[:tile], slope))
    up, down = both_ways(grad_pre, grad_pre, "h")

    place = jnp.stack([lax.axis_index("h"), core]).astype(jnp.int32)
    partial, hidden_all = joined_product(mine, other, weight_out, False, place)
    far_up, far_down = both_ways(up[:cut], down[cut:], "h")
    partial, far_up, far_down = lax.optimization_barrier((partial, far_up, far_down))
    output = rows_sum(partial)
    mine_late = stack(grad_pre, down, far_up, far_down, up)
    other_late = move(mine_late, "c", 1)
    partial, grad_pre_all = joined_product(mine_late, other_late, weight_in, True, place)
    input_grad = rows_sum(partial)
    weight_out_grad = across(hidden_all, grad_all).astype(BF16)
    weight_in_grad = across(input_all, grad_pre_all).astype(BF16)
    return (output, input_grad, weight_in_grad, weight_out_grad)


def solution(mesh):
    fine = Mesh(mesh.devices.reshape(4, 4, 2, 4, 2), ("x", "y", "l", "h", "c"))
    rows = P(("x", "y", "l"), ("h", "c"))
    columns = P(("h", "c"), ("x", "y", "l"))
    return jax.shard_map(
        on_device,
        mesh=fine,
        in_specs=(rows, columns, rows, rows),
        out_specs=(rows, rows, columns, rows),
        check_vma=False,
    )
```

```python
import functools

import jax
import jax.numpy as jnp
from jax import lax
from jax.experimental import pallas as pl
from jax.experimental.pallas import tpu as pltpu
from jax.sharding import Mesh, PartitionSpec as P

F32 = jnp.float32
BF16 = jnp.bfloat16
NEAR = ("x", "l")
FAR = ("y", "x", "l")
VMEM = 32 * 2**20


def gelu_both(value):
    inner = 0.7978845608 * (value + 0.044715 * value * value * value)
    tangent = jnp.tanh(inner)
    slope = 0.5 * (1.0 + tangent) + 0.5 * value * (1.0 - tangent * tangent) * 0.7978845608 * (
        1.0 + 0.134145 * value * value
    )
    return 0.5 * value * (1.0 + tangent), slope


def across(left, right):
    return lax.dot_general(left, right, (((0,), (0,)), ((), ())), preferred_element_type=F32)


def move(block, axis, hops):
    size = lax.axis_size(axis)
    return lax.ppermute(block, axis, [(i, (i + hops) % size) for i in range(size)])


def pick(array, index):
    return lax.dynamic_index_in_dim(array, index, 0, keepdims=False)


def ring_split(blocks, axis):
    spot = lax.axis_index(axis)
    own, ahead, far, behind = (pick(blocks, (spot + d) % 4) for d in range(4))
    return own, ahead, far.astype(BF16), behind


def both_ways(up, down, axis):
    return move(up, axis, 1), move(down, axis, -1)


def add_first(block, part):
    cut = part.shape[0]
    return jnp.concatenate([block[:cut] + part.astype(F32), block[cut:]], 0).astype(BF16)


def add_last(block, part):
    cut = block.shape[0] - part.shape[0]
    return jnp.concatenate([block[:cut], block[cut:] + part.astype(F32)], 0).astype(BF16)


def stack(*parts):
    return jnp.concatenate(parts, 0)


def ring_place(block, up, down, far_up, far_down, axis):
    spot = lax.axis_index(axis)
    cut = far_up.shape[0]
    whole = jnp.zeros((4,) + block.shape, block.dtype)
    for hops, piece in ((0, block), (3, up), (1, down)):
        whole = lax.dynamic_update_index_in_dim(whole, piece, (spot + hops) % 4, 0)
    far = (spot + 2) % 4
    whole = lax.dynamic_update_slice(whole, far_up[None], (far, 0, 0))
    return lax.dynamic_update_slice(whole, far_down[None], (far, cut, 0))


def product_kernel(turned, added, which_ref, rows_ref, weight_ref, *refs):
    out_ref = refs[-1]
    sides = ((1,), (1,)) if turned else ((1,), (0,))
    total = lax.dot_general(rows_ref[...], weight_ref[...], (sides, ((), ())), preferred_element_type=F32)
    if added:
        total = total + refs[0][...].astype(F32)
    out_ref[...] = total.astype(out_ref.dtype)


def product(rows, weight, turned, dtype, tile, which=None, weigh=1, later=(), plus=()):
    if which is None:
        stride, which = 1, jnp.zeros((1,), jnp.int32)
    else:
        stride, which = 2, which.astype(jnp.int32).reshape(1)
    steps = rows.shape[0] // tile // stride
    width = weight.shape[0] if turned else weight.shape[1]
    return pl.pallas_call(
        functools.partial(product_kernel, turned, len(plus) > 0),
        grid_spec=pltpu.PrefetchScalarGridSpec(
            num_scalar_prefetch=1,
            grid=(steps,),
            in_specs=[
                pl.BlockSpec((tile, rows.shape[1]), lambda i, which: (stride * i + which[0], 0)),
                pl.BlockSpec(weight.shape, lambda i, which: (0, 0)),
            ]
            + [pl.BlockSpec((tile, width), lambda i, which: (i, 0))] * len(plus)
            + [pl.BlockSpec(memory_space=pl.ANY)] * len(later),
            out_specs=pl.BlockSpec((tile, width), lambda i, which: (i, 0)),
        ),
        out_shape=jax.ShapeDtypeStruct((steps * tile, width), dtype),
        compiler_params=pltpu.CompilerParams(vmem_limit_bytes=VMEM),
        cost_estimate=pl.CostEstimate(
            flops=2 * weigh * steps * tile * weight.size,
            bytes_accessed=weigh * (2 * (steps * tile * rows.shape[1] + weight.size) + 4 * steps * tile * width),
            transcendentals=0,
        ),
    )(which, rows, weight, *plus, *later)


def joined_kernel(turned, place_ref, mine_ref, other_ref, weight_ref, *refs):
    out_ref, rows_ref = refs[-2:]
    sides = ((1,), (1,)) if turned else ((1,), (0,))
    rows_ref[...] = jnp.where(pl.program_id(0) % 2 == 0, mine_ref[...], other_ref[...])
    out_ref[...] = lax.dot_general(
        rows_ref[...], weight_ref[...], (sides, ((), ())), preferred_element_type=F32
    ).astype(out_ref.dtype)


def joined_product(mine, other, weight, turned, place, later=()):
    tile = mine.shape[0] // 4
    width = weight.shape[0] if turned else weight.shape[1]

    def spread(i, place):
        return (place[0] + i // 2) % 4 * 2 + (place[1] + i) % 2, 0

    return pl.pallas_call(
        functools.partial(joined_kernel, turned),
        grid_spec=pltpu.PrefetchScalarGridSpec(
            num_scalar_prefetch=1,
            grid=(8,),
            in_specs=[pl.BlockSpec((tile, mine.shape[1]), lambda i, place: (i // 2, 0))] * 2
            + [pl.BlockSpec(weight.shape, lambda i, place: (0, 0))]
            + [pl.BlockSpec(memory_space=pl.ANY)] * len(later),
            out_specs=[pl.BlockSpec((tile, width), spread), pl.BlockSpec((tile, mine.shape[1]), spread)],
        ),
        out_shape=[
            jax.ShapeDtypeStruct((8 * tile, width), BF16),
            jax.ShapeDtypeStruct((8 * tile, mine.shape[1]), BF16),
        ],
        compiler_params=pltpu.CompilerParams(vmem_limit_bytes=VMEM),
        cost_estimate=pl.CostEstimate(
            flops=16 * tile * weight.size,
            bytes_accessed=2 * (2 * mine.size + weight.size) + 16 * tile * (width + mine.shape[1]),
            transcendentals=0,
        ),
    )(place, mine, other, weight, *later)


def local(kernel, outs, args, later=(), flops=0):
    def body(*refs):
        kernel(*refs[: len(args)], *refs[len(args) + len(later) :])

    return pl.pallas_call(
        body,
        in_specs=[pl.BlockSpec(memory_space=pltpu.VMEM)] * len(args) + [pl.BlockSpec(memory_space=pl.ANY)] * len(later),
        out_specs=[pl.BlockSpec(memory_space=pltpu.VMEM)] * len(outs),
        out_shape=outs,
        compiler_params=pltpu.CompilerParams(vmem_limit_bytes=VMEM),
        cost_estimate=pl.CostEstimate(flops=flops, bytes_accessed=0, transcendentals=0) if flops else None,
    )(*args, *later)


def pass_on(ahead_ref, up_ref, behind_ref, down_ref, up_out, down_out):
    cut = up_ref.shape[0]
    up_out[:cut] = (ahead_ref[:cut] + up_ref[...].astype(F32)).astype(BF16)
    up_out[cut:] = ahead_ref[cut:].astype(BF16)
    down_out[:cut] = behind_ref[:cut].astype(BF16)
    down_out[cut:] = (behind_ref[cut:] + down_ref[...].astype(F32)).astype(BF16)


def activate(own_ref, up_ref, down_ref, hidden_ref, slope_ref):
    hidden, slope = gelu_both(own_ref[...] + up_ref[...].astype(F32) + down_ref[...].astype(F32))
    hidden_ref[...] = hidden.astype(BF16)
    slope_ref[...] = slope


def weigh_slope(own_ref, up_ref, down_ref, slope_ref, out_ref):
    total = own_ref[...] + up_ref[...].astype(F32) + down_ref[...].astype(F32)
    out_ref[...] = (total * slope_ref[...]).astype(BF16)


def on_device(inputs, weight_in, weight_out, output_grad):
    core = lax.axis_index("c")
    rows, features = inputs.shape
    near = lax.axis_size(NEAR)
    peers = lax.axis_size(FAR)
    tokens = peers * rows
    ring = lax.axis_size("h")
    tile = tokens // (2 * ring)

    def pair_sum(left, weight, turned, later=(), last=(), weigh=1):
        away = move(product(left, weight, turned, BF16, tile, 1 - core, weigh, later), "c", 1)
        total = product(left, weight, turned, F32, tile, core, weigh, last, (away,))
        return total.reshape(ring, tile, -1)

    def rows_sum(partial):
        pieces = lax.all_to_all(partial.reshape(peers, rows, -1), FAR, 0, 0)
        return pieces.astype(F32).sum(0).astype(BF16)

    def copies(block, axes):
        size = lax.axis_size(axes)
        sent = jnp.broadcast_to(block[None], (size,) + block.shape)
        return lax.all_to_all(sent, axes, 0, 0).reshape(size * rows, -1)

    def wire(count):
        return jax.ShapeDtypeStruct((count, units), BF16)

    units = weight_in.shape[1]
    cut = tile // 2
    input_all = copies(inputs, FAR)
    output_grad, input_all = lax.optimization_barrier((output_grad, input_all))
    grad = copies(output_grad, NEAR)

    own, ahead, far, behind = ring_split(pair_sum(input_all, weight_in, False), "h")
    up, down = both_ways(far[:cut], far[cut:], "h")
    grad_up, grad_down = both_ways(grad, grad, "y")
    ahead, behind = local(pass_on, [wire(tile)] * 2, (ahead, up, behind, down), (grad_up, grad_down))
    up, down = both_ways(ahead, behind, "h")
    part = grad.shape[0] // 2
    grad_far = both_ways(grad_up[:part], grad_down[part:], "y")
    hidden, slope = local(
        activate, [wire(tile), jax.ShapeDtypeStruct((tile, units), F32)], (own, up, down), (), 2 * 10**10
    )
    grad_all = ring_place(grad, grad_up, grad_down, *grad_far, "y").reshape(tokens, -1)

    own, ahead, far, behind = ring_split(pair_sum(grad_all, weight_out, True, (ahead, behind), (), 0), "h")
    up, down = both_ways(stack(hidden, far[:cut]), stack(hidden, far[cut:]), "h")
    ahead, behind = local(pass_on, [wire(tile)] * 2, (ahead, up[tile:], behind, down[tile:]))
    far_up, far_down = both_ways(stack(ahead, up[:cut]), stack(behind, down[cut:tile]), "h")
    mine = stack(hidden, down[:tile], far_up[tile:], far_down[tile:], up[:tile])
    other = move(mine, "c", 1)
    (grad_pre,) = local(weigh_slope, [wire(tile)], (own, far_up[:tile], far_down[:tile], slope))
    up, down = both_ways(grad_pre, grad_pre, "h")

    place = jnp.stack([lax.axis_index("h"), core]).astype(jnp.int32)
    partial, hidden_all = joined_product(mine, other, weight_out, False, place)
    far_up, far_down = both_ways(up[:cut], down[cut:], "h")
    partial, far_up, far_down = lax.optimization_barrier((partial, far_up, far_down))
    output = rows_sum(partial)
    mine_late = stack(grad_pre, down, far_up, far_down, up)
    other_late = move(mine_late, "c", 1)
    partial, grad_pre_all = joined_product(mine_late, other_late, weight_in, True, place)
    input_grad = rows_sum(partial)
    weight_out_grad = across(hidden_all, grad_all).astype(BF16)
    weight_in_grad = across(input_all, grad_pre_all).astype(BF16)
    return (output, input_grad, weight_in_grad, weight_out_grad)


def solution(mesh):
    fine = Mesh(mesh.devices.reshape(4, 4, 2, 4, 2), ("x", "y", "l", "h", "c"))
    rows = P(("x", "y", "l"), ("h", "c"))
    columns = P(("h", "c"), ("x", "y", "l"))
    return jax.shard_map(
        on_device,
        mesh=fine,
        in_specs=(rows, columns, rows, rows),
        out_specs=(rows, rows, columns, rows),
        check_vma=False,
    )
```
